128 devices in a mesh: heads: 8 (over x, y_hi), blk: 16 (over z, y_lo, core).
Axes of the slice: x: 4, y: 4 (y_hi: 2, y_lo: 2; y = y_hi * 2 + y_lo), z: 4, core: 2. Of those that a mesh axis runs over, the one named last changes fastest.
Arguments:
- queries: bfloat16 [32768, 64, 128], P(('blk', 'heads')), may hold values from -22 to 22
- key_states: bfloat16 [32768, 8, 128], P(('blk', 'heads')), may hold values from -4 to 4
- value_states: bfloat16 [32768, 8, 128], P(('blk', 'heads')), may hold values from -6 to 6
- block_lists: int32 [256, 64, 8], P(('blk', 'heads')), may hold values from 0 to 255, as said below
Outputs:
- attended: bfloat16 [32768, 64, 128], P(('blk', 'heads'))
The draws below stay inside these ranges and needn't reach their ends.
Inputs may be any that keep to these rules, and one draw needn't show every extreme that they name: block_lists[j, h] holds 8 distinct blocks, each in the shard of 16 blocks that holds j or in the shard before it; j itself is always listed; every query block outside the first shard lists at least one block of the shard before; over the query blocks of one shard and the 8 query heads of one key head, exactly 4 distinct blocks of the shard before are listed (none for the first shard).
All inputs are finite; a program needn't handle non-finite values.
Results may differ from the reference program's by a relative error of at most 0.0049.
Values may be sent and summed in bfloat16 or wider, within the bound.
No kernel may reach another device: no remote copies, remote signals or barrier semaphores. Data moves between devices by JAX's collectives and lax.ppermute only.
A program may use at most 128 MiB of HBM per device.

```python
import jax
import jax.numpy as jnp
from jax import lax

QHEADS = 64
KVHEADS = 8
HEAD_DIM = 128
BLOCK = 128
LISTED = 8
REMOTE = 4
SEQ = 32768
SHARD_BLOCKS = 16
QBLOCKS = 256


def draw_queries(key, part):
    key = jax.random.fold_in(key, 11)
    return jax.random.truncated_normal(key, -4.0, 4.0, (SEQ, QHEADS, HEAD_DIM), jnp.float32).astype(jnp.bfloat16)


def draw_key_states(key, part):
    key = jax.random.fold_in(key, 23)
    return jax.random.truncated_normal(key, -4.0, 4.0, (SEQ, KVHEADS, HEAD_DIM), jnp.float32).astype(jnp.bfloat16)


def draw_block_lists(key, part):
    key = jax.random.fold_in(key, 5)
    chosen_key, order_key, shuffle_key = jax.random.split(key, 3)
    shards = QBLOCKS // SHARD_BLOCKS
    sharing = QHEADS // KVHEADS
    pool = SHARD_BLOCKS + REMOTE
    chosen = jax.vmap(lambda sub_key: jax.random.permutation(sub_key, SHARD_BLOCKS))(jax.random.split(chosen_key, shards * KVHEADS)).reshape(shards, KVHEADS, SHARD_BLOCKS)[:, :, :REMOTE]
    rank_scores = jax.vmap(lambda sub_key: jax.random.permutation(sub_key, pool))(jax.random.split(order_key, QBLOCKS * QHEADS)).reshape(QBLOCKS, QHEADS, pool)
    rows = jnp.arange(QBLOCKS, dtype=jnp.int32)
    shard_of = rows // SHARD_BLOCKS
    within = rows % SHARD_BLOCKS
    slots = jnp.arange(pool, dtype=jnp.int32)
    head_group = jnp.arange(QHEADS, dtype=jnp.int32) // sharing
    remote_local = chosen[jnp.maximum(shard_of - 1, 0)][:, head_group, :]
    own_ids = jnp.broadcast_to((shard_of[:, None] * SHARD_BLOCKS + jnp.arange(SHARD_BLOCKS, dtype=jnp.int32))[:, None, :], (QBLOCKS, QHEADS, SHARD_BLOCKS))
    remote_ids = (shard_of - 1)[:, None, None] * SHARD_BLOCKS + remote_local
    candidates = jnp.concatenate([own_ids, remote_ids], axis=-1)
    first_shard = (shard_of == 0)[:, None, None]
    scores = rank_scores + jnp.where(first_shard & (slots >= SHARD_BLOCKS), pool, 0)
    scores = jnp.where(slots == within[:, None, None], -2, scores)
    scores = jnp.where(jnp.logical_not(first_shard) & (slots == SHARD_BLOCKS + within[:, None, None] % REMOTE), -1, scores)
    order = jnp.argsort(scores, axis=-1, stable=True)[..., :LISTED]
    picked = jnp.take_along_axis(candidates, order, axis=-1)
    shuffle = jax.vmap(lambda sub_key: jax.random.permutation(sub_key, LISTED))(jax.random.split(shuffle_key, QBLOCKS * QHEADS)).reshape(QBLOCKS, QHEADS, LISTED)
    return jnp.take_along_axis(picked, shuffle, axis=-1).astype(jnp.int32)


def level_of(own_key, extent, pieces, least, largest):
    def one(position, shards_of):
        draws = jax.random.uniform(jax.random.fold_in(jax.random.fold_in(own_key, 6), position), (shards_of,), jnp.float32, least / len(pieces), largest / len(pieces))
        return jnp.repeat(jnp.exp(draws), extent[position] // shards_of).reshape((-1,) + (1,) * (len(extent) - position - 1))

    factor_of = one(*pieces[0])
    for cut in pieces[1:]:
        factor_of = factor_of * one(*cut)
    return factor_of


def bell_draw(key, shape, spread, most, cuts=(), kind=jnp.bfloat16):
    values = spread * jax.random.normal(key, shape, jnp.float32)
    if cuts:
        values = values * level_of(key, shape, cuts, -0.22, 0.18)
    return jnp.clip(values, -most, most).astype(kind)


def setup_inputs(seed: int = 0) -> dict:
    key_list = jax.random.split(jax.random.key(seed), 5)
    queries = draw_queries(jax.random.fold_in(key_list[4], 71), 0)
    key_states = draw_key_states(jax.random.fold_in(key_list[4], 71), 0)
    value_states = bell_draw(key_list[2], (SEQ, KVHEADS, HEAD_DIM), 1.0, 6.0, ((0, 128),))
    block_lists = draw_block_lists(jax.random.fold_in(key_list[4], 71), 0)
    return {"queries": queries, "key_states": key_states, "value_states": value_states, "block_lists": block_lists}


def attend_blocks(query_rows, key_table, value_table, listing):
    members = listing.shape[0]
    picked_keys = key_table[listing].reshape(members, -1, key_table.shape[-1]).astype(jnp.float32)
    picked_values = value_table[listing].reshape(members, -1, value_table.shape[-1]).astype(jnp.float32)
    scores = jnp.einsum("qbd,qkd->qbk", query_rows.astype(jnp.float32), picked_keys) * (query_rows.shape[-1] ** -0.5)
    highest = jnp.max(scores, axis=-1, keepdims=True)
    powers = jnp.exp(scores - highest)
    totals = jnp.sum(powers, axis=-1, keepdims=True)
    weights = lax.optimization_barrier((powers / totals).astype(jnp.bfloat16))
    mixed = jnp.einsum("qbk,qkd->qbd", weights.astype(jnp.float32), picked_values)
    return mixed.astype(jnp.bfloat16)


def reference(queries, key_states, value_states, block_lists):
    sharing = QHEADS // KVHEADS
    shards = QBLOCKS // SHARD_BLOCKS

    def one_head(head):
        query_rows = lax.dynamic_index_in_dim(queries, head, 1, keepdims=False).reshape(shards, SHARD_BLOCKS, BLOCK, HEAD_DIM)
        key_table = lax.dynamic_index_in_dim(key_states, head // sharing, 1, keepdims=False).reshape(QBLOCKS, BLOCK, HEAD_DIM)
        value_table = lax.dynamic_index_in_dim(value_states, head // sharing, 1, keepdims=False).reshape(QBLOCKS, BLOCK, HEAD_DIM)
        listing = lax.dynamic_index_in_dim(block_lists, head, 1, keepdims=False).reshape(shards, SHARD_BLOCKS, LISTED)

        def one_shard(pair):
            return attend_blocks(pair[0], key_table, value_table, pair[1])

        return lax.map(one_shard, (query_rows, listing)).reshape(SEQ, HEAD_DIM)

    stacked = lax.map(one_head, jnp.arange(QHEADS, dtype=jnp.int32))
    return jnp.transpose(stacked, (1, 0, 2))
```

```python
import functools
import math

import jax
import jax.numpy as jnp
from jax import lax
from jax.experimental import pallas as pl
from jax.experimental.pallas import tpu as pltpu
from jax.sharding import PartitionSpec as P

BLOCK = 128
WIDTH = 128
SHARD_BLOCKS = 16
REMOTE = 4
LISTED = 8
KV = 8
SHARING = 8
LOCAL = 2
ROWS = LOCAL * BLOCK
PIECES = 8
CHUNKS = (3, 3, 2)
FACTOR = math.log2(math.e) / math.sqrt(WIDTH)
NT = (((1,), (1,)), ((), ()))

X_UP = [(i, (i + 2) % 8) for i in range(8)]
X_DOWN = [(i, (i - 2) % 8) for i in range(8)]
Y_SWAP = [(i, i ^ 1) for i in range(8)]


def over_heads(array, route):
    return lax.ppermute(array, "heads", route)


def split_kernel(keys, values, *rest):
    outs, wide = rest[:-1], rest[-1]
    for which, source in enumerate((keys, values)):
        wide[...] = source[...].astype(jnp.float32).reshape(ROWS * KV, WIDTH)
        head = 0
        for out in outs:
            for place in range(out.shape[1]):
                rows = wide[pl.ds(head, ROWS, stride=KV), :]
                out[which, place] = rows.astype(jnp.bfloat16)
                head += 1


def split_heads(keys, values):
    return pl.pallas_call(
        split_kernel,
        out_shape=[jax.ShapeDtypeStruct((2, size, ROWS, WIDTH), jnp.bfloat16) for size in CHUNKS],
        scratch_shapes=[pltpu.VMEM((ROWS * KV, WIDTH), jnp.float32)],
        name="split_heads",
    )(keys, values)


def pick_kernel(places, *refs):
    pieces, out, sems = refs[:PIECES], refs[PIECES], refs[PIECES + 1]
    size = out.shape[1]

    def copy(piece, head, slot, half):
        return pltpu.make_async_copy(
            piece.at[:, head, pl.ds(half * BLOCK, BLOCK), :],
            out.at[:, head, pl.ds(slot * BLOCK, BLOCK), :],
            sems.at[head, slot],
        )

    for head in range(size):
        for slot in range(REMOTE):
            place = places[head * REMOTE + slot]
            for number in range(PIECES):

                @pl.when(place // LOCAL == number)
                def _():
                    copy(pieces[number], head, slot, place % LOCAL).start()

    for head in range(size):
        for slot in range(REMOTE):
            copy(pieces[0], head, slot, 0).wait()


def pick_blocks(places, pieces):
    size = pieces[0].shape[1]
    anywhere = pl.BlockSpec(memory_space=pl.ANY)
    return pl.pallas_call(
        pick_kernel,
        out_shape=jax.ShapeDtypeStruct((2, size, REMOTE * BLOCK, WIDTH), jnp.bfloat16),
        in_specs=[pl.BlockSpec(memory_space=pltpu.SMEM)] + [anywhere] * PIECES,
        out_specs=anywhere,
        scratch_shapes=[pltpu.SemaphoreType.DMA((size, REMOTE))],
        cost_estimate=pl.CostEstimate(flops=0, bytes_accessed=size * 2**20, transcendentals=0),
        name="pick_blocks",
    )(places, *pieces)


def attend_kernel(first, aliased, slots, *refs):
    pieces, picked = refs[:PIECES], refs[PIECES]
    queries = refs[PIECES + 1]
    out, table, wide, mixed = refs[PIECES + 2 + aliased :]
    head, block = pl.program_id(0), pl.program_id(1)

    @pl.when(block == 0)
    def _():
        for number, piece in enumerate(pieces):
            table[:, pl.ds(number * ROWS, ROWS), :] = piece[:, 0]
        table[:, pl.ds(PIECES * ROWS, REMOTE * BLOCK), :] = picked[:, 0]

    wide[...] = queries[...].astype(jnp.float32).reshape(BLOCK * SHARING, WIDTH)
    base = (block * KV + first + head) * (SHARING * LISTED)

    def two(which, member, pair):
        at = [slots[base + member * LISTED + 2 * pair + i] for i in range(2)]
        return jnp.concatenate(
            [table[which, pl.ds(pl.multiple_of(s * BLOCK, BLOCK), BLOCK), :] for s in at], 0
        )

    def scores_of(member):
        rows = wide[pl.ds(member, BLOCK, stride=SHARING), :].astype(jnp.bfloat16)
        return [
            lax.dot_general(rows, two(0, member, pair), NT, preferred_element_type=jnp.float32)
            for pair in range(LISTED // 2)
        ]

    def powers_of(scores):
        highest = jnp.max(functools.reduce(jnp.maximum, scores), axis=1, keepdims=True)
        powers = [jnp.exp2((part - highest) * FACTOR) for part in scores]
        totals = jnp.sum(functools.reduce(jnp.add, powers), axis=1, keepdims=True)
        return [part.astype(jnp.bfloat16) for part in powers], totals

    def mix(member, powers, totals):
        total = jnp.zeros((BLOCK, WIDTH), jnp.float32)
        for pair in range(LISTED // 2):
            total += jnp.dot(powers[pair], two(1, member, pair), preferred_element_type=jnp.float32)
        mixed[pl.ds(member, BLOCK, stride=SHARING), :] = total * (1.0 / totals)

    scores, before = scores_of(0), None
    for member in range(SHARING):
        later = scores_of(member + 1) if member + 1 < SHARING else None
        now = powers_of(scores)
        if before is not None:
            mix(member - 1, *before)
        before, scores = now, later
    mix(SHARING - 1, *before)
    out[...] = mixed[...].reshape(BLOCK, SHARING, WIDTH).astype(jnp.bfloat16)


def attend(first, slots, pieces, picked, queries, earlier):
    size = pieces[0].shape[1]
    aliased = earlier is not None
    per_head = lambda rows: pl.BlockSpec((2, 1, rows, WIDTH), lambda head, block, _: (0, head, 0, 0))
    per_block = pl.BlockSpec(
        (BLOCK, SHARING, WIDTH), lambda head, block, _: (block, first + head, 0)
    )
    return pl.pallas_call(
        functools.partial(attend_kernel, first, aliased),
        grid_spec=pltpu.PrefetchScalarGridSpec(
            num_scalar_prefetch=1,
            grid=(size, LOCAL),
            in_specs=[per_head(ROWS)] * PIECES
            + [per_head(REMOTE * BLOCK), per_block]
            + [pl.BlockSpec(memory_space=pl.ANY)] * aliased,
            out_specs=per_block,
            scratch_shapes=[
                pltpu.VMEM((2, (SHARD_BLOCKS + REMOTE) * BLOCK, WIDTH), jnp.bfloat16),
                pltpu.VMEM((BLOCK * SHARING, WIDTH), jnp.float32),
                pltpu.VMEM((BLOCK * SHARING, WIDTH), jnp.float32),
            ],
        ),
        out_shape=jax.ShapeDtypeStruct(queries.shape, queries.dtype),
        input_output_aliases={PIECES + 3: 0} if aliased else {},
        compiler_params=pltpu.CompilerParams(vmem_limit_bytes=24 * 2**20),
        cost_estimate=pl.CostEstimate(
            flops=size * 2 * 2 * 2**30, bytes_accessed=size * 4 * 2**20, transcendentals=size * 2**21
        ),
        name=f"attend_{first}",
    )(slots, *pieces, picked, queries, *([earlier] if aliased else []))


def on_device(queries, key_states, value_states, block_lists):
    shard, member = lax.axis_index("blk"), lax.axis_index("heads")
    mine_x, mine_y = member // 2, member % 2
    own = split_heads(key_states, value_states)

    def place_of(block):
        across = (block // 4 - mine_x) % 4
        return across * 4 + ((block // 2) % 2 ^ mine_y) * 2 + block % 2

    local = (block_lists - (shard - 1) * SHARD_BLOCKS).reshape(LOCAL, KV, SHARING, LISTED)
    behind = jnp.arange(SHARD_BLOCKS, dtype=jnp.int32)
    listed = (local[..., None] == behind).any((0, 2, 3))
    rank = jnp.sum(listed[:, None, :] & (behind[None, :] < behind[:, None]), -1, dtype=jnp.int32)
    wanted = jnp.sum(
        jnp.where(
            listed[:, None, :] & (rank[:, None, :] == jnp.arange(REMOTE, dtype=jnp.int32)[:, None]),
            behind,
            0,
        ),
        -1,
        dtype=jnp.int32,
    )
    asked = lax.ppermute(wanted, "blk", [(i + 1, i) for i in range(lax.axis_size("blk") - 1)])
    ranks = jnp.sum(
        listed[None, :, None, None, :] & (behind < local[..., None]), -1, dtype=jnp.int32
    )
    slots = jnp.where(
        local >= SHARD_BLOCKS, place_of(local - SHARD_BLOCKS), SHARD_BLOCKS + ranks
    ).reshape(-1)
    places = place_of(asked).reshape(-1)
    onward = [(i, i + 1) for i in range(lax.axis_size("blk") - 1)]

    result, first = None, 0
    for a in own:
        size = a.shape[1]
        b = over_heads(a, Y_SWAP)
        a_down, a_up = over_heads(a, X_UP), over_heads(a, X_DOWN)
        b_down, b_up = over_heads(b, X_UP), over_heads(b, X_DOWN)
        a_far, b_far = over_heads(a_down, X_UP), over_heads(b_up, X_DOWN)
        pieces = [a, b, a_up, b_up, a_far, b_far, a_down, b_down]
        chosen = pick_blocks(places[first * REMOTE : (first + size) * REMOTE], pieces)
        picked = lax.ppermute(chosen, "blk", onward)
        result = attend(first, slots, pieces, picked, queries, result)
        first += size
    return result


def solution(mesh):
    spec = P(("blk", "heads"), None, None)
    return jax.shard_map(
        on_device,
        mesh=mesh,
        in_specs=(spec,) * 4,
        out_specs=spec,
        check_vma=False,
    )
```

```python
import functools
import math

import jax
import jax.numpy as jnp
from jax import lax
from jax.experimental import pallas as pl
from jax.experimental.pallas import tpu as pltpu
from jax.sharding import PartitionSpec as P

BLOCK = 128
WIDTH = 128
SHARD_BLOCKS = 16
REMOTE = 4
LISTED = 8
KV = 8
SHARING = 8
LOCAL = 2
ROWS = LOCAL * BLOCK
PIECES = 8
EARLY, CROSS, LATE = 2, 2, 4
GROUPS = ((0, EARLY + CROSS), (0, EARLY), (EARLY + CROSS, KV))
FACTOR = math.log2(math.e) / math.sqrt(WIDTH)
NT = (((1,), (1,)), ((), ()))

X_UP = [(i, (i + 2) % 8) for i in range(8)]
X_DOWN = [(i, (i - 2) % 8) for i in range(8)]
Y_SWAP = [(i, i ^ 1) for i in range(8)]


def over_heads(array, route):
    return lax.ppermute(array, "heads", route)


def split_kernel(keys, values, *rest):
    outs, wide = rest[:-1], rest[-1]
    for which, source in enumerate((keys, values)):
        wide[...] = source[...].astype(jnp.float32).reshape(ROWS * KV, WIDTH)
        for head in range(KV):
            rows = wide[pl.ds(head, ROWS, stride=KV), :].astype(jnp.bfloat16)
            for out, (first, last) in zip(outs, GROUPS):
                if first <= head < last:
                    out[which, head - first] = rows


def split_heads(keys, values):
    return pl.pallas_call(
        split_kernel,
        out_shape=[
            jax.ShapeDtypeStruct((2, last - first, ROWS, WIDTH), jnp.bfloat16)
            for first, last in GROUPS
        ],
        scratch_shapes=[pltpu.VMEM((ROWS * KV, WIDTH), jnp.float32)],
        cost_estimate=pl.CostEstimate(flops=1, bytes_accessed=1, transcendentals=0),
        name="split_heads",
    )(keys, values)


def plan_kernel(where, lists, table, wanted):
    base, mine_x, mine_y = where[0], where[1], where[2]
    table[KV * 2 * SHARD_BLOCKS] = base

    def place_of(number):
        across = (number // 4 - mine_x) & 3
        return across * 4 + ((number // 2) % 2 ^ mine_y) * 2 + number % 2

    places = [place_of(number) for number in range(SHARD_BLOCKS)]

    def one_head(head, carry):
        mask = jnp.int32(0)
        for block in range(LOCAL):
            for member in range(SHARING):
                for entry in range(LISTED):
                    local = lists[block, entry, head * SHARING + member] - base
                    bit = lax.shift_left(jnp.int32(1), jnp.minimum(local, SHARD_BLOCKS))
                    mask = mask | bit
        for slot in range(REMOTE):
            wanted[head * REMOTE + slot] = 0
        count = jnp.int32(0)
        for number in range(SHARD_BLOCKS):
            table[head * 2 * SHARD_BLOCKS + number] = SHARD_BLOCKS + count
            listed = lax.shift_right_logical(mask, jnp.int32(number)) & 1

            @pl.when(listed == 1)
            def _():
                wanted[head * REMOTE + count] = places[number]

            count = count + listed
            table[head * 2 * SHARD_BLOCKS + SHARD_BLOCKS + number] = places[number]
        return carry

    lax.fori_loop(0, KV, one_head, 0)


def plan(where, lists):
    scalars = pl.BlockSpec(memory_space=pltpu.SMEM)
    return pl.pallas_call(
        plan_kernel,
        out_shape=[
            jax.ShapeDtypeStruct((KV * 2 * SHARD_BLOCKS + 1,), jnp.int32),
            jax.ShapeDtypeStruct((KV * REMOTE,), jnp.int32),
        ],
        in_specs=[scalars, scalars],
        out_specs=[scalars, scalars],
        cost_estimate=pl.CostEstimate(flops=1, bytes_accessed=1, transcendentals=0),
        name="plan",
    )(where, lists)


def join(table, pieces, head):
    if len(pieces) == PIECES:
        for number, piece in enumerate(pieces):
            table[:, pl.ds(number * ROWS, ROWS), :] = piece[:, head]
    else:
        for across in range(4):
            for number, piece in enumerate(pieces):
                table[:, pl.ds((2 * across + number) * ROWS, ROWS), :] = piece[across, :, head]


def per_head(array, within=0):
    if array.ndim == 5:
        return pl.BlockSpec((4, 2, 1, ROWS, WIDTH), lambda head, *_: (0, 0, within + head, 0, 0))
    return pl.BlockSpec((2, 1, array.shape[2], WIDTH), lambda head, *_: (0, within + head, 0, 0))


def pick_kernel(first, within, asked, *refs):
    pieces, (out, joined) = refs[:-2], refs[-2:]
    head = within + pl.program_id(0)
    join(joined, pieces, head)
    head = first + head
    for slot in range(REMOTE):
        place = asked[head * REMOTE + slot]
        rows = pl.ds(pl.multiple_of(place * BLOCK, BLOCK), BLOCK)
        out[:, 0, pl.ds(slot * BLOCK, BLOCK), :] = joined[:, rows, :]


def pick_blocks(first, within, size, asked, pieces):
    return pl.pallas_call(
        functools.partial(pick_kernel, first, within),
        grid_spec=pltpu.PrefetchScalarGridSpec(
            num_scalar_prefetch=1,
            grid=(size,),
            in_specs=[pl.BlockSpec(memory_space=pltpu.VMEM)] * len(pieces),
            out_specs=pl.BlockSpec(
                (2, 1, REMOTE * BLOCK, WIDTH), lambda head, *_: (0, head, 0, 0)
            ),
            scratch_shapes=[pltpu.VMEM((2, SHARD_BLOCKS * BLOCK, WIDTH), jnp.bfloat16)],
        ),
        out_shape=jax.ShapeDtypeStruct((2, size, REMOTE * BLOCK, WIDTH), jnp.bfloat16),
        cost_estimate=pl.CostEstimate(flops=1, bytes_accessed=1, transcendentals=0),
        compiler_params=pltpu.CompilerParams(vmem_limit_bytes=16 * 2**20),
        name=f"pick_blocks_{first + within}",
    )(asked, *pieces)


def attend_kernel(first, within, picked_within, aliased, lists, places, *refs):
    out, table, wide, mixed = refs[-4:]
    *pieces, picked, queries = refs[: -4 - aliased]
    head, block = pl.program_id(0), pl.program_id(1)

    @pl.when(block == 0)
    def _():
        join(table, pieces, within + head)
        table[:, pl.ds(PIECES * ROWS, REMOTE * BLOCK), :] = picked[:, picked_within + head]

    wide[...] = queries[...].astype(jnp.float32).reshape(BLOCK * SHARING, WIDTH)
    base, group = places[KV * 2 * SHARD_BLOCKS], first + within + head

    def slot_of(member, entry):
        local = lists[block, entry, group * SHARING + member] - base
        return places[group * 2 * SHARD_BLOCKS + local]

    def two(which, member, pair):
        at = [slot_of(member, 2 * pair + i) for i in range(2)]
        return jnp.concatenate(
            [table[which, pl.ds(pl.multiple_of(s * BLOCK, BLOCK), BLOCK), :] for s in at], 0
        )

    def scores_of(member):
        rows = wide[pl.ds(member, BLOCK, stride=SHARING), :].astype(jnp.bfloat16)
        return [
            lax.dot_general(rows, two(0, member, pair), NT, preferred_element_type=jnp.float32)
            for pair in range(LISTED // 2)
        ]

    def powers_of(scores):
        highest = jnp.max(functools.reduce(jnp.maximum, scores), axis=1, keepdims=True)
        powers = [jnp.exp2((part - highest) * FACTOR) for part in scores]
        totals = jnp.sum(functools.reduce(jnp.add, powers), axis=1, keepdims=True)
        return [part.astype(jnp.bfloat16) for part in powers], totals

    def mix(member, powers, totals):
        total = jnp.zeros((BLOCK, WIDTH), jnp.float32)
        for pair in range(LISTED // 2):
            total += jnp.dot(powers[pair], two(1, member, pair), preferred_element_type=jnp.float32)
        mixed[pl.ds(member, BLOCK, stride=SHARING), :] = total * (1.0 / totals)

    scores, before = scores_of(0), None
    for member in range(SHARING):
        later = scores_of(member + 1) if member + 1 < SHARING else None
        now = powers_of(scores)
        if before is not None:
            mix(member - 1, *before)
        before, scores = now, later
    mix(SHARING - 1, *before)
    out[...] = mixed[...].reshape(BLOCK, SHARING, WIDTH).astype(jnp.bfloat16)


def attend(first, within, size, scalars, pieces, picked, picked_within, queries, earlier):
    aliased = earlier is not None
    per_block = pl.BlockSpec(
        (BLOCK, SHARING, WIDTH), lambda head, block, *_: (block, first + within + head, 0)
    )
    return pl.pallas_call(
        functools.partial(attend_kernel, first, within, picked_within, aliased),
        grid_spec=pltpu.PrefetchScalarGridSpec(
            num_scalar_prefetch=2,
            grid=(size, LOCAL),
            in_specs=[pl.BlockSpec(memory_space=pltpu.VMEM)] * (len(pieces) + 1)
            + [per_block]
            + [pl.BlockSpec(memory_space=pl.ANY)] * aliased,
            out_specs=per_block,
            scratch_shapes=[
                pltpu.VMEM((2, (SHARD_BLOCKS + REMOTE) * BLOCK, WIDTH), jnp.bfloat16),
                pltpu.VMEM((BLOCK * SHARING, WIDTH), jnp.float32),
                pltpu.VMEM((BLOCK * SHARING, WIDTH), jnp.float32),
            ],
        ),
        out_shape=jax.ShapeDtypeStruct(queries.shape, queries.dtype),
        input_output_aliases={len(pieces) + 4: 0} if aliased else {},
        compiler_params=pltpu.CompilerParams(vmem_limit_bytes=16 * 2**20),
        cost_estimate=pl.CostEstimate(
            flops=size * 2**30, bytes_accessed=1, transcendentals=0
        ),
        name=f"attend_{first + within}",
    )(*scalars, *pieces, picked, queries, *([earlier] if aliased else []))


def after(array, *others):
    return lax.optimization_barrier((array, *others))[0]


def on_device(queries, key_states, value_states, block_lists):
    shard, member = lax.axis_index("blk"), lax.axis_index("heads")
    where = jnp.stack([(shard - 1) * SHARD_BLOCKS, member // 2, member % 2]).astype(jnp.int32)
    lists = jnp.transpose(block_lists, (0, 2, 1))
    most, early, late = split_heads(key_states, value_states)
    table, wanted = plan(where, lists)
    shards = lax.axis_size("blk")
    asked = lax.ppermute(wanted, "blk", [(i + 1, i) for i in range(shards - 1)])

    def fetch(first, within, size, pieces):
        chosen = pick_blocks(first, within, size, asked, pieces)
        return lax.ppermute(chosen, "blk", [(i, i + 1) for i in range(shards - 1)])

    def heads(first, within, size, pieces, arrived, earlier):
        return attend(first, within, size, (lists, table), pieces, arrived, 0, queries, earlier)

    swapped = over_heads(early, Y_SWAP)
    down, up = over_heads(most, X_UP), over_heads(most, X_DOWN)
    done = (swapped, down, up, asked)

    swapped = after(swapped, *done)
    swapped_down, swapped_up = over_heads(swapped, X_UP), over_heads(swapped, X_DOWN)
    half = CROSS // 2
    far = over_heads(after(down[:, : EARLY + half], *done), X_UP)
    far_rest = over_heads(after(up[:, EARLY + half :], *done), X_DOWN)
    late_swapped = over_heads(after(late, *done), Y_SWAP)
    row = jnp.stack(
        [
            most[:, EARLY:],
            up[:, EARLY:],
            jnp.concatenate([far[:, EARLY:], far_rest], 1),
            down[:, EARLY:],
        ]
    )
    done = (swapped_down, swapped_up, far, late_swapped, row)

    swapped_far = over_heads(swapped_up, X_DOWN)
    cross = [row, over_heads(after(row, *done), Y_SWAP)]
    late_down, late_up = (over_heads(after(late, *done), route) for route in (X_UP, X_DOWN))
    first = [most, swapped, up, swapped_up, far, swapped_far, down, swapped_down]
    arrived = fetch(0, 0, EARLY, first)

    late_swapped = after(late_swapped, late_down, late_up, swapped_far)
    late_swapped_down, late_swapped_up = (
        over_heads(late_swapped, route) for route in (X_UP, X_DOWN)
    )
    result = heads(0, 0, EARLY, first, after(arrived, late_down, late_up), None)
    done = (late_down, late_up, late_swapped_down, late_swapped_up)

    late_far = over_heads(after(late_down, *done), X_UP)
    late_swapped_far = over_heads(after(late_swapped_up, *done), X_DOWN)
    arrived = fetch(EARLY, 0, CROSS, cross)
    result = heads(EARLY, 0, CROSS, cross, arrived, result)

    last = [late, late_swapped, late_up, late_swapped_up]
    last += [after(late_far, result), late_swapped_far, late_down, late_swapped_down]
    begin, half = EARLY + CROSS, LATE // 2
    arrived = [fetch(begin, 0, half, last), fetch(begin, half, LATE - half, last)]
    result = heads(begin, 0, half, last, arrived[0], result)
    return heads(begin, half, LATE - half, last, arrived[1], result)


def solution(mesh):
    spec = P(("blk", "heads"), None, None)
    return jax.shard_map(
        on_device,
        mesh=mesh,
        in_specs=(spec,) * 4,
        out_specs=spec,
        check_vma=False,
    )
```

```python
import functools
import math

import jax
import jax.numpy as jnp
from jax import lax
from jax.experimental import pallas as pl
from jax.experimental.pallas import tpu as pltpu
from jax.sharding import PartitionSpec as P

BLOCK = 128
WIDTH = 128
SHARD_BLOCKS = 16
REMOTE = 4
LISTED = 8
KV = 8
SHARING = 8
LOCAL = 2
ROWS = LOCAL * BLOCK
PIECES = 8
EARLY, CROSS, LATE = 2, 2, 4
GROUPS = ((0, EARLY + CROSS), (0, EARLY), (EARLY + CROSS, KV))
FACTOR = math.log2(math.e) / math.sqrt(WIDTH)
NT = (((1,), (1,)), ((), ()))

X_UP = [(i, (i + 2) % 8) for i in range(8)]
X_DOWN = [(i, (i - 2) % 8) for i in range(8)]
Y_SWAP = [(i, i ^ 1) for i in range(8)]


def over_heads(array, route):
    return lax.ppermute(array, "heads", route)


def split_kernel(keys, values, *rest):
    outs, wide = rest[:-1], rest[-1]
    for which, source in enumerate((keys, values)):
        wide[...] = source[...].astype(jnp.float32).reshape(ROWS * KV, WIDTH)
        for head in range(KV):
            rows = wide[pl.ds(head, ROWS, stride=KV), :].astype(jnp.bfloat16)
            for out, (first, last) in zip(outs, GROUPS):
                if first <= head < last:
                    out[which, head - first] = rows


def split_heads(keys, values):
    return pl.pallas_call(
        split_kernel,
        out_shape=[
            jax.ShapeDtypeStruct((2, last - first, ROWS, WIDTH), jnp.bfloat16)
            for first, last in GROUPS
        ],
        scratch_shapes=[pltpu.VMEM((ROWS * KV, WIDTH), jnp.float32)],
        cost_estimate=pl.CostEstimate(flops=1, bytes_accessed=1, transcendentals=0),
        name="split_heads",
    )(keys, values)


def plan_kernel(where, lists, table, wanted):
    base, mine_x, mine_y = where[0], where[1], where[2]
    table[KV * 2 * SHARD_BLOCKS] = base

    def place_of(number):
        across = (number // 4 - mine_x) & 3
        return across * 4 + ((number // 2) % 2 ^ mine_y) * 2 + number % 2

    places = [place_of(number) for number in range(SHARD_BLOCKS)]

    def one_head(head, carry):
        mask = jnp.int32(0)
        for block in range(LOCAL):
            for member in range(SHARING):
                for entry in range(LISTED):
                    local = lists[block, entry, head * SHARING + member] - base
                    bit = lax.shift_left(jnp.int32(1), jnp.minimum(local, SHARD_BLOCKS))
                    mask = mask | bit
        for slot in range(REMOTE):
            wanted[head * REMOTE + slot] = 0
        count = jnp.int32(0)
        for number in range(SHARD_BLOCKS):
            table[head * 2 * SHARD_BLOCKS + number] = SHARD_BLOCKS + count
            listed = lax.shift_right_logical(mask, jnp.int32(number)) & 1

            @pl.when(listed == 1)
            def _():
                wanted[head * REMOTE + count] = places[number]

            count = count + listed
            table[head * 2 * SHARD_BLOCKS + SHARD_BLOCKS + number] = places[number]
        return carry

    lax.fori_loop(0, KV, one_head, 0)


def plan(where, lists):
    scalars = pl.BlockSpec(memory_space=pltpu.SMEM)
    return pl.pallas_call(
        plan_kernel,
        out_shape=[
            jax.ShapeDtypeStruct((KV * 2 * SHARD_BLOCKS + 1,), jnp.int32),
            jax.ShapeDtypeStruct((KV * REMOTE,), jnp.int32),
        ],
        in_specs=[scalars, scalars],
        out_specs=[scalars, scalars],
        cost_estimate=pl.CostEstimate(flops=1, bytes_accessed=1, transcendentals=0),
        name="plan",
    )(where, lists)


def join(table, pieces, begins, head):
    if len(pieces) == PIECES:
        for number, (piece, begin) in enumerate(zip(pieces, begins)):
            table[:, pl.ds(number * ROWS, ROWS), :] = piece[:, begin + head]
    else:
        for across in range(4):
            for number, piece in enumerate(pieces):
                table[:, pl.ds((2 * across + number) * ROWS, ROWS), :] = piece[across, :, head]


def pick_kernel(first, begins, asked, *refs):
    pieces, (out, joined) = refs[:-2], refs[-2:]
    head = pl.program_id(0)
    join(joined, pieces, begins, head)
    head = first + head
    for slot in range(REMOTE):
        place = asked[head * REMOTE + slot]
        rows = pl.ds(pl.multiple_of(place * BLOCK, BLOCK), BLOCK)
        out[:, 0, pl.ds(slot * BLOCK, BLOCK), :] = joined[:, rows, :]


def pick_blocks(first, size, asked, pieces, begins):
    return pl.pallas_call(
        functools.partial(pick_kernel, first, begins),
        grid_spec=pltpu.PrefetchScalarGridSpec(
            num_scalar_prefetch=1,
            grid=(size,),
            in_specs=[pl.BlockSpec(memory_space=pltpu.VMEM)] * len(pieces),
            out_specs=pl.BlockSpec(
                (2, 1, REMOTE * BLOCK, WIDTH), lambda head, *_: (0, head, 0, 0)
            ),
            scratch_shapes=[pltpu.VMEM((2, SHARD_BLOCKS * BLOCK, WIDTH), jnp.bfloat16)],
        ),
        out_shape=jax.ShapeDtypeStruct((2, size, REMOTE * BLOCK, WIDTH), jnp.bfloat16),
        cost_estimate=pl.CostEstimate(flops=1, bytes_accessed=1, transcendentals=0),
        compiler_params=pltpu.CompilerParams(vmem_limit_bytes=16 * 2**20),
        name=f"pick_blocks_{first}",
    )(asked, *pieces)


def attend_kernel(first, begins, aliased, lists, places, *refs):
    out, table, wide, mixed = refs[-4:]
    *pieces, picked, queries = refs[: -4 - aliased]
    head = pl.program_id(0)
    join(table, pieces, begins, head)
    table[:, pl.ds(PIECES * ROWS, REMOTE * BLOCK), :] = picked[:, head]
    wide[...] = queries[...].astype(jnp.float32).reshape(ROWS * SHARING, WIDTH)
    base, group = places[KV * 2 * SHARD_BLOCKS], first + head

    def slot_of(member, entry):
        block, member = divmod(member, SHARING)
        local = lists[block, entry, group * SHARING + member] - base
        return places[group * 2 * SHARD_BLOCKS + local]

    def two(which, member, pair):
        at = [slot_of(member, 2 * pair + i) for i in range(2)]
        return jnp.concatenate(
            [table[which, pl.ds(pl.multiple_of(s * BLOCK, BLOCK), BLOCK), :] for s in at], 0
        )

    def rows_of(member):
        block, member = divmod(member, SHARING)
        return pl.ds(block * BLOCK * SHARING + member, BLOCK, stride=SHARING)

    def scores_of(member):
        rows = wide[rows_of(member), :].astype(jnp.bfloat16)
        return [
            lax.dot_general(rows, two(0, member, pair), NT, preferred_element_type=jnp.float32)
            for pair in range(LISTED // 2)
        ]

    def powers_of(scores):
        highest = jnp.max(functools.reduce(jnp.maximum, scores), axis=1, keepdims=True)
        powers = [jnp.exp2((part - highest) * FACTOR) for part in scores]
        totals = jnp.sum(functools.reduce(jnp.add, powers), axis=1, keepdims=True)
        return [part.astype(jnp.bfloat16) for part in powers], totals

    def mix(member, powers, totals):
        total = jnp.zeros((BLOCK, WIDTH), jnp.float32)
        for pair in range(LISTED // 2):
            total += jnp.dot(powers[pair], two(1, member, pair), preferred_element_type=jnp.float32)
        mixed[rows_of(member), :] = total * (1.0 / totals)

    scores, before = scores_of(0), None
    for member in range(LOCAL * SHARING):
        later = scores_of(member + 1) if member + 1 < LOCAL * SHARING else None
        now = powers_of(scores)
        if before is not None:
            mix(member - 1, *before)
        before, scores = now, later
    mix(LOCAL * SHARING - 1, *before)
    out[...] = mixed[...].reshape(ROWS, SHARING, WIDTH).astype(jnp.bfloat16)


def attend(first, size, scalars, pieces, begins, picked, queries, earlier):
    aliased = earlier is not None
    per_group = pl.BlockSpec((ROWS, SHARING, WIDTH), lambda head, *_: (0, first + head, 0))
    return pl.pallas_call(
        functools.partial(attend_kernel, first, begins, aliased),
        grid_spec=pltpu.PrefetchScalarGridSpec(
            num_scalar_prefetch=2,
            grid=(size,),
            in_specs=[pl.BlockSpec(memory_space=pltpu.VMEM)] * (len(pieces) + 1)
            + [per_group]
            + [pl.BlockSpec(memory_space=pl.ANY)] * aliased,
            out_specs=per_group,
            scratch_shapes=[
                pltpu.VMEM((2, (SHARD_BLOCKS + REMOTE) * BLOCK, WIDTH), jnp.bfloat16),
                pltpu.VMEM((ROWS * SHARING, WIDTH), jnp.float32),
                pltpu.VMEM((ROWS * SHARING, WIDTH), jnp.float32),
            ],
        ),
        out_shape=jax.ShapeDtypeStruct(queries.shape, queries.dtype),
        input_output_aliases={len(pieces) + 4: 0} if aliased else {},
        compiler_params=pltpu.CompilerParams(vmem_limit_bytes=16 * 2**20),
        cost_estimate=pl.CostEstimate(
            flops=size * 2**30, bytes_accessed=1, transcendentals=0
        ),
        name=f"attend_{first}",
    )(*scalars, *pieces, picked, queries, *([earlier] if aliased else []))


def after(array, *others):
    return lax.optimization_barrier((array, *others))[0]


def on_device(queries, key_states, value_states, block_lists):
    shard, member = lax.axis_index("blk"), lax.axis_index("heads")
    where = jnp.stack([(shard - 1) * SHARD_BLOCKS, member // 2, member % 2]).astype(jnp.int32)
    lists = jnp.transpose(block_lists, (0, 2, 1))
    most, early, late = split_heads(key_states, value_states)
    table, wanted = plan(where, lists)
    shards = lax.axis_size("blk")
    asked = lax.ppermute(wanted, "blk", [(i + 1, i) for i in range(shards - 1)])

    def choose(first, size, pieces, begins=(0,) * PIECES):
        return pick_blocks(first, size, asked, pieces, begins)

    def send(chosen):
        return lax.ppermute(chosen, "blk", [(i, i + 1) for i in range(shards - 1)])

    def heads(first, size, pieces, arrived, earlier, begins=(0,) * PIECES):
        return attend(first, size, (lists, table), pieces, begins, arrived, queries, earlier)

    swapped = over_heads(early, Y_SWAP)
    down, up = over_heads(most, X_UP), over_heads(most, X_DOWN)
    done = (swapped, down, up, asked)

    swapped = after(swapped, *done)
    swapped_down, swapped_up = over_heads(swapped, X_UP), over_heads(swapped, X_DOWN)
    half = CROSS // 2
    far = over_heads(after(down[:, : EARLY + half], *done), X_UP)
    far_rest = over_heads(after(up[:, EARLY + half :], *done), X_DOWN)
    late_swapped = over_heads(after(late, *done), Y_SWAP)
    row = jnp.stack(
        [
            most[:, EARLY:],
            up[:, EARLY:],
            jnp.concatenate([far[:, EARLY:], far_rest], 1),
            down[:, EARLY:],
        ]
    )
    swapped_far = over_heads(swapped_up, X_DOWN)
    done = (swapped_down, far, late_swapped, row, swapped_far)
    first = [most, swapped, up, swapped_up, far, swapped_far, down, swapped_down]
    chosen = choose(0, EARLY, first)
    arrived = send(chosen)

    cross = [row, over_heads(after(row, chosen), Y_SWAP)]
    late_down, late_up = (over_heads(after(late, *done), route) for route in (X_UP, X_DOWN))
    late_swapped_down, late_swapped_up = (
        over_heads(after(late_swapped, *done), route) for route in (X_UP, X_DOWN)
    )
    result = heads(0, EARLY, first, arrived, None)

    done = (late_down, late_up, late_swapped_down, late_swapped_up, result)
    late_far = over_heads(after(late_down, *done), X_UP)
    late_swapped_far = over_heads(after(late_swapped_up, *done), X_DOWN)
    cross[1] = after(cross[1], result)
    cross_arrived = send(choose(EARLY, CROSS, cross))
    last = [late, late_swapped, late_up, late_swapped_up]
    last += [late_far, late_swapped_far, late_down, late_swapped_down]
    begin, half = EARLY + CROSS, LATE // 2
    chosen = choose(begin, half, last)
    begins = (half,) * PIECES
    chosen_more = choose(begin + half, LATE - half, last, begins)
    result = heads(EARLY, CROSS, cross, after(cross_arrived, chosen, chosen_more), result)
    result = heads(begin, half, last, send(chosen), result)
    return heads(begin + half, LATE - half, last, send(chosen_more), result, begins)


def solution(mesh):
    spec = P(("blk", "heads"), None, None)
    return jax.shard_map(
        on_device,
        mesh=mesh,
        in_specs=(spec,) * 4,
        out_specs=spec,
        check_vma=False,
    )
```

```python
import functools
import math

import jax
import jax.numpy as jnp
from jax import lax
from jax.experimental import pallas as pl
from jax.experimental.pallas import tpu as pltpu
from jax.sharding import PartitionSpec as P

BLOCK = 128
WIDTH = 128
SHARD_BLOCKS = 16
REMOTE = 4
LISTED = 8
KV = 8
SHARING = 8
LOCAL = 2
ROWS = LOCAL * BLOCK
PIECES = 8
EARLY, CROSS, LATE = 2, 2, 4
GROUPS = ((0, EARLY + CROSS), (0, EARLY), (EARLY + CROSS, KV))
FACTOR = math.log2(math.e) / math.sqrt(WIDTH)
NT = (((1,), (1,)), ((), ()))

X_UP = [(i, (i + 2) % 8) for i in range(8)]
X_DOWN = [(i, (i - 2) % 8) for i in range(8)]
Y_SWAP = [(i, i ^ 1) for i in range(8)]


def over_heads(array, route):
    return lax.ppermute(array, "heads", route)


def split_kernel(keys, values, *rest):
    outs, wide = rest[:-1], rest[-1]
    for which, source in enumerate((keys, values)):
        wide[...] = source[...].astype(jnp.float32).reshape(ROWS * KV, WIDTH)
        for head in range(KV):
            rows = wide[pl.ds(head, ROWS, stride=KV), :].astype(jnp.bfloat16)
            for out, (first, last) in zip(outs, GROUPS):
                if first <= head < last:
                    out[which, head - first] = rows


def split_heads(keys, values):
    return pl.pallas_call(
        split_kernel,
        out_shape=[
            jax.ShapeDtypeStruct((2, last - first, ROWS, WIDTH), jnp.bfloat16)
            for first, last in GROUPS
        ],
        scratch_shapes=[pltpu.VMEM((ROWS * KV, WIDTH), jnp.float32)],
        cost_estimate=pl.CostEstimate(flops=1, bytes_accessed=1, transcendentals=0),
        name="split_heads",
    )(keys, values)


def plan_kernel(where, lists, table, wanted):
    base, mine_x, mine_y = where[0], where[1], where[2]
    table[KV * 2 * SHARD_BLOCKS] = base

    def place_of(number):
        across = (number // 4 - mine_x) & 3
        return across * 4 + ((number // 2) % 2 ^ mine_y) * 2 + number % 2

    places = [place_of(number) for number in range(SHARD_BLOCKS)]

    def one_head(head, carry):
        mask = jnp.int32(0)
        for block in range(LOCAL):
            for member in range(SHARING):
                for entry in range(LISTED):
                    local = lists[block, entry, head * SHARING + member] - base
                    bit = lax.shift_left(jnp.int32(1), jnp.minimum(local, SHARD_BLOCKS))
                    mask = mask | bit
        for slot in range(REMOTE):
            wanted[head * REMOTE + slot] = 0
        count = jnp.int32(0)
        for number in range(SHARD_BLOCKS):
            table[head * 2 * SHARD_BLOCKS + number] = SHARD_BLOCKS + count
            listed = lax.shift_right_logical(mask, jnp.int32(number)) & 1

            @pl.when(listed == 1)
            def _():
                wanted[head * REMOTE + count] = places[number]

            count = count + listed
            table[head * 2 * SHARD_BLOCKS + SHARD_BLOCKS + number] = places[number]
        return carry

    lax.fori_loop(0, KV, one_head, 0)


def plan(where, lists):
    scalars = pl.BlockSpec(memory_space=pltpu.SMEM)
    return pl.pallas_call(
        plan_kernel,
        out_shape=[
            jax.ShapeDtypeStruct((KV * 2 * SHARD_BLOCKS + 1,), jnp.int32),
            jax.ShapeDtypeStruct((KV * REMOTE,), jnp.int32),
        ],
        in_specs=[scalars, scalars],
        out_specs=[scalars, scalars],
        cost_estimate=pl.CostEstimate(flops=1, bytes_accessed=1, transcendentals=0),
        name="plan",
    )(where, lists)


def join(table, pieces, begins, head):
    if len(pieces) == PIECES:
        for number, (piece, begin) in enumerate(zip(pieces, begins)):
            table[:, pl.ds(number * ROWS, ROWS), :] = piece[:, begin + head]
    else:
        for across in range(4):
            for number, piece in enumerate(pieces):
                table[:, pl.ds((2 * across + number) * ROWS, ROWS), :] = piece[across, :, head]


def pick_kernel(first, begins, asked, *refs):
    pieces, (out, joined) = refs[:-2], refs[-2:]
    head = pl.program_id(0)
    join(joined, pieces, begins, head)
    head = first + head
    for slot in range(REMOTE):
        place = asked[head * REMOTE + slot]
        rows = pl.ds(pl.multiple_of(place * BLOCK, BLOCK), BLOCK)
        out[:, 0, pl.ds(slot * BLOCK, BLOCK), :] = joined[:, rows, :]


def pick_blocks(first, size, asked, pieces, begins):
    return pl.pallas_call(
        functools.partial(pick_kernel, first, begins),
        grid_spec=pltpu.PrefetchScalarGridSpec(
            num_scalar_prefetch=1,
            grid=(size,),
            in_specs=[pl.BlockSpec(memory_space=pltpu.VMEM)] * len(pieces),
            out_specs=pl.BlockSpec(
                (2, 1, REMOTE * BLOCK, WIDTH), lambda head, *_: (0, head, 0, 0)
            ),
            scratch_shapes=[pltpu.VMEM((2, SHARD_BLOCKS * BLOCK, WIDTH), jnp.bfloat16)],
        ),
        out_shape=jax.ShapeDtypeStruct((2, size, REMOTE * BLOCK, WIDTH), jnp.bfloat16),
        cost_estimate=pl.CostEstimate(flops=1, bytes_accessed=1, transcendentals=0),
        compiler_params=pltpu.CompilerParams(vmem_limit_bytes=8 * 2**20),
        name=f"pick_blocks_{first}",
    )(asked, *pieces)


def attend_kernel(first, begins, aliased, lists, places, *refs):
    out, table, wide, mixed = refs[-4:]
    *pieces, picked, queries = refs[: -4 - aliased]
    head = pl.program_id(0)
    join(table, pieces, begins, head)
    table[:, pl.ds(PIECES * ROWS, REMOTE * BLOCK), :] = picked[:, head]
    wide[...] = queries[...].astype(jnp.float32).reshape(ROWS * SHARING, WIDTH)
    base, group = places[KV * 2 * SHARD_BLOCKS], first + head

    def slot_of(member, entry):
        block, member = divmod(member, SHARING)
        local = lists[block, entry, group * SHARING + member] - base
        return places[group * 2 * SHARD_BLOCKS + local]

    def two(which, member, pair):
        at = [slot_of(member, 2 * pair + i) for i in range(2)]
        return jnp.concatenate(
            [table[which, pl.ds(pl.multiple_of(s * BLOCK, BLOCK), BLOCK), :] for s in at], 0
        )

    def rows_of(member):
        block, member = divmod(member, SHARING)
        return pl.ds(block * BLOCK * SHARING + member, BLOCK, stride=SHARING)

    def scores_of(member):
        rows = wide[rows_of(member), :].astype(jnp.bfloat16)
        return [
            lax.dot_general(rows, two(0, member, pair), NT, preferred_element_type=jnp.float32)
            for pair in range(LISTED // 2)
        ]

    def powers_of(scores):
        highest = jnp.max(functools.reduce(jnp.maximum, scores), axis=1, keepdims=True)
        powers = [jnp.exp2((part - highest) * FACTOR) for part in scores]
        totals = jnp.sum(functools.reduce(jnp.add, powers), axis=1, keepdims=True)
        return [part.astype(jnp.bfloat16) for part in powers], totals

    def mix(member, powers, totals):
        total = jnp.zeros((BLOCK, WIDTH), jnp.float32)
        for pair in range(LISTED // 2):
            total += jnp.dot(powers[pair], two(1, member, pair), preferred_element_type=jnp.float32)
        mixed[rows_of(member), :] = total * (1.0 / totals)

    scores, before = scores_of(0), None
    for member in range(LOCAL * SHARING):
        later = scores_of(member + 1) if member + 1 < LOCAL * SHARING else None
        now = powers_of(scores)
        if before is not None:
            mix(member - 1, *before)
        before, scores = now, later
    mix(LOCAL * SHARING - 1, *before)
    out[...] = mixed[...].reshape(ROWS, SHARING, WIDTH).astype(jnp.bfloat16)


def attend(first, size, scalars, pieces, begins, picked, queries, earlier):
    aliased = earlier is not None
    per_group = pl.BlockSpec((ROWS, SHARING, WIDTH), lambda head, *_: (0, first + head, 0))
    return pl.pallas_call(
        functools.partial(attend_kernel, first, begins, aliased),
        grid_spec=pltpu.PrefetchScalarGridSpec(
            num_scalar_prefetch=2,
            grid=(size,),
            in_specs=[pl.BlockSpec(memory_space=pltpu.VMEM)] * (len(pieces) + 1)
            + [per_group]
            + [pl.BlockSpec(memory_space=pl.ANY)] * aliased,
            out_specs=per_group,
            scratch_shapes=[
                pltpu.VMEM((2, (SHARD_BLOCKS + REMOTE) * BLOCK, WIDTH), jnp.bfloat16),
                pltpu.VMEM((ROWS * SHARING, WIDTH), jnp.float32),
                pltpu.VMEM((ROWS * SHARING, WIDTH), jnp.float32),
            ],
        ),
        out_shape=jax.ShapeDtypeStruct(queries.shape, queries.dtype),
        input_output_aliases={len(pieces) + 4: 0} if aliased else {},
        compiler_params=pltpu.CompilerParams(vmem_limit_bytes=16 * 2**20),
        cost_estimate=pl.CostEstimate(
            flops=size * 2**30, bytes_accessed=1, transcendentals=0
        ),
        name=f"attend_{first}",
    )(*scalars, *pieces, picked, queries, *([earlier] if aliased else []))


def after(array, *others):
    return lax.optimization_barrier((array, *others))[0]


def on_device(queries, key_states, value_states, block_lists):
    shard, member = lax.axis_index("blk"), lax.axis_index("heads")
    where = jnp.stack([(shard - 1) * SHARD_BLOCKS, member // 2, member % 2]).astype(jnp.int32)
    lists = jnp.transpose(block_lists, (0, 2, 1))
    most, early, late = split_heads(key_states, value_states)
    table, wanted = plan(where, lists)
    shards = lax.axis_size("blk")
    asked = lax.ppermute(wanted, "blk", [(i + 1, i) for i in range(shards - 1)])

    def choose(first, size, pieces, begins=(0,) * PIECES):
        return pick_blocks(first, size, asked, pieces, begins)

    def send(chosen):
        return lax.ppermute(chosen, "blk", [(i, i + 1) for i in range(shards - 1)])

    def heads(first, size, pieces, arrived, earlier, begins=(0,) * PIECES):
        return attend(first, size, (lists, table), pieces, begins, arrived, queries, earlier)

    swapped = over_heads(early, Y_SWAP)
    down, up = over_heads(most, X_UP), over_heads(most, X_DOWN)
    done = (swapped, down, up, asked)

    swapped = after(swapped, *done)
    swapped_down, swapped_up = over_heads(swapped, X_UP), over_heads(swapped, X_DOWN)
    half = CROSS // 2
    far = over_heads(after(down[:, : EARLY + half], *done), X_UP)
    far_rest = over_heads(after(up[:, EARLY + half :], *done), X_DOWN)
    late_swapped = over_heads(after(late, *done), Y_SWAP)
    row = jnp.stack(
        [
            most[:, EARLY:],
            up[:, EARLY:],
            jnp.concatenate([far[:, EARLY:], far_rest], 1),
            down[:, EARLY:],
        ]
    )
    swapped_far = over_heads(swapped_up, X_DOWN)
    done = (swapped_down, far, late_swapped, row, swapped_far)
    first = [most, swapped, up, swapped_up, far, swapped_far, down, swapped_down]
    chosen = choose(0, EARLY, first)
    arrived = send(chosen)

    cross = [row, over_heads(after(row, chosen), Y_SWAP)]
    late_down, late_up = (over_heads(after(late, *done), route) for route in (X_UP, X_DOWN))
    late_swapped_down, late_swapped_up = (
        over_heads(after(late_swapped, *done), route) for route in (X_UP, X_DOWN)
    )
    result = heads(0, EARLY, first, arrived, None)

    done = (late_down, late_up, late_swapped_down, late_swapped_up, result)
    late_far = over_heads(after(late_down, *done), X_UP)
    late_swapped_far = over_heads(after(late_swapped_up, *done), X_DOWN)
    cross[1] = after(cross[1], result)
    cross_arrived = send(choose(EARLY, CROSS, cross))
    last = [late, late_swapped, late_up, late_swapped_up]
    last += [late_far, late_swapped_far, late_down, late_swapped_down]
    begin, half = EARLY + CROSS, LATE // 2
    chosen = choose(begin, half, last)
    begins = (half,) * PIECES
    chosen_more = choose(begin + half, LATE - half, last, begins)
    result = heads(EARLY, CROSS, cross, after(cross_arrived, chosen, chosen_more), result)
    result = heads(begin, half, last, send(chosen), result)
    return heads(begin + half, LATE - half, last, send(chosen_more), result, begins)


def solution(mesh):
    spec = P(("blk", "heads"), None, None)
    return jax.shard_map(
        on_device,
        mesh=mesh,
        in_specs=(spec,) * 4,
        out_specs=spec,
        check_vma=False,
    )
```
